32 devices in a mesh: blk: 4 (over y, core), rep: 8 (over z, x).
Axes of the slice: x: 2, y: 2, z: 4, core: 2. Of those that a mesh axis runs over, the one named last changes fastest.
Arguments:
- grad_out: bfloat16 [4096, 256], P(('blk', 'rep')), may hold values from -6 to 6
- relu_bits: int32 [4096, 256], P(('blk', 'rep')), may hold values 0 or 1
- features: bfloat16 [4096, 256], P(('blk', 'rep')), may hold values from -6 to 6
- weight: bfloat16 [256, 256], replicated, may hold values from -0.375 to 0.375
- tiles: bfloat16 [32, 4, 2, 128, 128], P(('blk', 'rep')), as said below
- tile_rows: int32 [32, 4, 2], P(('blk', 'rep')), may hold values from 0 to 7
- tile_counts: int32 [32, 4], P(('blk', 'rep')), may hold values from 1 to 2, as said below
Outputs:
- grad_features: bfloat16 [4096, 256], P(('blk', 'rep'))
- grad_weight: float32 [256, 256], replicated
The draws below stay inside these ranges and needn't reach their ends.
Inputs may be any that keep to these rules, and one draw needn't show every extreme that they name: `tile_counts`: for every sub-block, some source block has exactly 2 nonzero tiles; loads differ between sub-blocks. `tiles`: about one entry in eight of a tile is nonzero.
All inputs are finite; a program needn't handle non-finite values. No bound on the sum of `relu_bits` on one device may be relied on, other than what follows from the above.
Results may differ from the reference program's by a relative error of at most 0.005.
Values may be sent and summed in bfloat16 or wider, within the bound.
A program may use at most 64 MiB of HBM per device.

```python
import jax
import jax.numpy as jnp
from jax import lax

F = 256
TILE = 128
ROWS_DEV = 128
MAXT = 2
BLOCK_TILES = 8
NODES = 4096
N_BLK = 4
N_REP = 8


def draw_tile_counts(key, part):
    base_key = jax.random.fold_in(key, 7)
    key_one, key_two, key_three = jax.random.split(base_key, 3)
    shape = (N_BLK * N_REP, N_BLK)
    raw = jax.random.randint(key_one, shape, 1, MAXT + 1)
    limit = jax.random.randint(key_three, (N_BLK * N_REP, 1), 1, MAXT + 1)
    base = jnp.minimum(raw, limit)
    where_full = jax.random.randint(key_two, (N_BLK * N_REP, 1), 0, N_BLK)
    column = jnp.arange(N_BLK, dtype=jnp.int32)[None, :]
    return jnp.where(column == where_full, MAXT, base).astype(jnp.int32)


def draw_tiles(key, part):
    base_key = jax.random.fold_in(key, 11)
    key_vals, key_mask = jax.random.split(base_key, 2)
    shape = (N_BLK * N_REP, N_BLK, MAXT, ROWS_DEV, TILE)
    values = jax.random.normal(key_vals, shape, jnp.float32)
    keep = jax.random.randint(key_mask, shape, 0, 8) == 0
    scale = (N_BLK * MAXT * TILE / 16.0) ** (-0.5)
    return jnp.where(keep, values * scale, jnp.zeros_like(values)).astype(jnp.bfloat16)


def place_ends(drawn, rng, low, high):
    index_at = [jax.random.randint(jax.random.fold_in(rng, axis), (), 0, length) for axis, length in enumerate(drawn.shape)]
    widest = drawn.shape.index(max(drawn.shape))
    neighbour = index_at[:widest] + [(index_at[widest] + 1) % drawn.shape[widest]] + index_at[widest + 1:]
    return drawn.at[tuple(index_at)].set(low).at[tuple(neighbour)].set(high)


def steps_of(own_key, shape, cuts, least, top_value):
    loudness = 1.0
    for dim, shards_of in cuts:
        steps = jax.random.uniform(jax.random.fold_in(jax.random.fold_in(own_key, 6), dim), (shards_of,), jnp.float32, least / len(cuts), top_value / len(cuts))
        loudness = loudness * jnp.repeat(jnp.exp(steps), shape[dim] // shards_of).reshape((-1,) + (1,) * (len(shape) - 1 - dim))
    return loudness


def bell_draw(stream_key, dims, deviation, most, cuts=(), held_as=jnp.bfloat16):
    result = jax.random.normal(stream_key, dims, jnp.float32) * deviation
    if len(cuts) > 0:
        result = steps_of(stream_key, dims, cuts, -0.22, 0.18) * result
    return jnp.clip(result, min=-most, max=most).astype(held_as)


def setup_inputs(seed: int = 0) -> dict:
    seeds = jax.random.split(jax.random.key(seed), 8)
    return {
        "grad_out": bell_draw(seeds[0], (NODES, F), 1.0, 6.0, ((0, 32),)),
        "relu_bits": place_ends((jax.random.randint(seeds[1], (NODES, F), 0, 2) < 1).astype(jnp.int32), jax.random.fold_in(seeds[1], 1), 0, 1),
        "features": bell_draw(seeds[2], (NODES, F), 1.0, 6.0, ((0, 32),)),
        "weight": bell_draw(seeds[3], (F, F), F ** -0.5, 0.375),
        "tiles": draw_tiles(jax.random.fold_in(seeds[7], 71), 0),
        "tile_rows": place_ends(jax.random.randint(seeds[5], (N_BLK * N_REP, N_BLK, MAXT), 0, BLOCK_TILES), jax.random.fold_in(seeds[5], 1), 0, BLOCK_TILES - 1).astype(jnp.int32),
        "tile_counts": draw_tile_counts(jax.random.fold_in(seeds[7], 71), 0),
    }


def reference(grad_out, relu_bits, features, weight, tiles, tile_rows, tile_counts):
    masked = jnp.where(relu_bits == 1, grad_out, jnp.zeros_like(grad_out)).astype(jnp.bfloat16)
    masked_sub = masked.reshape(N_BLK, N_REP, ROWS_DEV, F)
    total = jnp.zeros((N_BLK, BLOCK_TILES, TILE, F), jnp.float32)
    slots = jnp.arange(MAXT, dtype=jnp.int32)

    def per_device(device, total):
        block_id = (device // N_REP).astype(jnp.int32)
        sub_id = (device % N_REP).astype(jnp.int32)

        def per_source(source, total):
            piece = masked_sub[source, sub_id].astype(jnp.float32)
            tile_set = tiles[device, source].astype(jnp.float32)
            prods = jnp.einsum("krt,rf->ktf", tile_set, piece)
            live = (slots < tile_counts[device, source])[:, None, None]
            prods = jnp.where(live, prods, jnp.zeros_like(prods))
            return total.at[block_id, tile_rows[device, source]].add(prods)

        return lax.fori_loop(0, N_BLK, per_source, total)

    total = lax.fori_loop(0, N_BLK * N_REP, per_device, total)
    aggregated = total.reshape(NODES, F).astype(jnp.bfloat16)
    grad_features = jnp.dot(aggregated, weight.T, preferred_element_type=jnp.float32).astype(jnp.bfloat16)
    grad_weight = jnp.dot(features.T, aggregated, preferred_element_type=jnp.float32) * (NODES ** -0.5)
    return grad_features, grad_weight
```

```python
import functools

import jax
import jax.numpy as jnp
from jax import lax
from jax.experimental import pallas as pl
from jax.experimental.pallas import tpu as pltpu
from jax.sharding import PartitionSpec as P

MESH = pl.DeviceIdType.MESH
UNROLL = 8
GROUP = 4


def loop(low, high, step):
    if high - low <= UNROLL:
        for index in range(low, high):
            step(index)
    else:
        lax.fori_loop(low, high, lambda index, carry: (step(index), carry)[1], 0)


def fold(count, step, start):
    if count <= UNROLL:
        for index in range(count):
            start = step(index, start)
        return start
    return lax.fori_loop(0, count, step, start)


def remote(source, target, send, receive, device):
    return pltpu.make_async_remote_copy(
        src_ref=source,
        dst_ref=target,
        send_sem=send,
        recv_sem=receive,
        device_id=device,
        device_id_type=MESH,
    )


def kernel(
    nblk, nrep, scale,
    rows_ref, counts_ref, grad_ref, relu_ref, feat_ref, weight_ref, tiles_ref,
    gf_ref, gw_ref,
    pieces, turned, feat_t, away, arrived, own, terms, terms_low, share_in, block_sum, final,
    gs, gr, rs, rr, ts, tr, bs, br, fs, fr,
):
    me_b = lax.axis_index("blk")
    me_r = lax.axis_index("rep")
    slot_count = tiles_ref.shape[2]
    rows = terms.shape[1]
    halves = gw_ref.shape[1] // 128
    per_half = nrep // halves

    barrier = pltpu.get_barrier_semaphore()

    def greet_b(d):
        pl.semaphore_signal(barrier, inc=1, device_id={"blk": lax.rem(me_b + d, nblk)}, device_id_type=MESH)

    def greet_r(e):
        pl.semaphore_signal(barrier, inc=1, device_id={"rep": lax.rem(me_r + e, nrep)}, device_id_type=MESH)

    loop(1, nblk, greet_b)
    loop(1, nrep, greet_r)
    grad = grad_ref[...]
    pieces[0] = jnp.where(relu_ref[...] == 1, grad, jnp.zeros_like(grad))
    pl.semaphore_wait(barrier, nblk + nrep - 2)

    def gather(d):
        return remote(pieces.at[0], pieces.at[d], gs.at[d], gr.at[d], {"blk": lax.rem(me_b + d, nblk)})

    loop(1, nblk, lambda d: gather(d).start())

    def turn(d):
        source = lax.rem(me_b - d + nblk, nblk)
        for k in range(slot_count):
            turned[d, k] = tiles_ref[0, source, k].T

    loop(0, nblk, turn)
    feat_t[...] = feat_ref[...].T
    loop(1, nblk, lambda d: gather(d).wait_recv())

    def partial(t):
        def part(g, total):
            right = pieces[pl.ds(g * GROUP, GROUP)].reshape(GROUP * pieces.shape[1], pieces.shape[2])
            for k in range(slot_count):
                left = []
                for i in range(GROUP):
                    d = g * GROUP + i
                    source = lax.rem(me_b - d + nblk, nblk)
                    live = (rows_ref[0, source, k] == t) & (k < counts_ref[0, source])
                    here = turned[d, k]
                    gate = jnp.full((1, here.shape[1]), live.astype(jnp.float32)).astype(here.dtype)
                    left.append(here * gate)
                total = total + jnp.dot(jnp.concatenate(left, axis=1), right, preferred_element_type=jnp.float32)
            return total

        return fold(nblk // GROUP, part, jnp.zeros(own.shape, jnp.float32))

    def scatter(e):
        return remote(away.at[e], arrived.at[e], rs.at[e], rr.at[e], {"rep": lax.rem(me_r + e, nrep)})

    def send_part(e):
        away[e] = partial(lax.rem(me_r + e, nrep)).astype(away.dtype)
        scatter(e).start()

    loop(1, nrep, send_part)
    own[...] = partial(me_r)

    def take(e):
        scatter(e).wait_recv()
        own[...] += arrived[e].astype(jnp.float32)

    loop(1, nrep, take)
    aggregated = own[...].astype(jnp.bfloat16)

    term = jnp.dot(feat_t[...], aggregated, preferred_element_type=jnp.float32) * scale
    for p in range(nrep):
        half, at = p // per_half, (p % per_half) * rows
        cut = term[at:at + rows, half * 128:half * 128 + 128]
        terms[p] = cut
        terms_low[p] = cut.astype(terms_low.dtype)

    def share(e):
        other = lax.rem(me_r + e, nrep)
        return remote(terms_low.at[other], share_in.at[e], ts.at[e], tr.at[e], {"rep": other})

    loop(1, nrep, lambda e: share(e).start())
    gf_ref[...] = lax.dot_general(
        aggregated, weight_ref[...], (((1,), (1,)), ((), ())), preferred_element_type=jnp.float32
    ).astype(gf_ref.dtype)

    def take_share(index, total):
        e = index + 1
        share(e).wait_recv()
        return total + share_in[e].astype(jnp.float32)

    block_sum[me_b] = fold(nrep - 1, take_share, terms[me_r]).astype(block_sum.dtype)

    def across(d):
        return remote(block_sum.at[me_b], block_sum.at[me_b], bs.at[d], br.at[d], {"blk": lax.rem(me_b + d, nblk)})

    loop(1, nblk, lambda d: across(d).start())
    loop(1, nblk, lambda d: across(d).wait_recv())
    whole = fold(nblk, lambda b, total: total + block_sum[b].astype(jnp.float32), jnp.zeros(terms.shape[1:], jnp.float32))
    final[me_r] = whole.astype(final.dtype)

    def spread(e):
        return remote(final.at[me_r], final.at[me_r], fs.at[e], fr.at[e], {"rep": lax.rem(me_r + e, nrep)})

    loop(1, nrep, lambda e: spread(e).start())
    loop(1, nrep, lambda e: spread(e).wait_recv())
    for p in range(nrep):
        half, at = p // per_half, (p % per_half) * rows
        gw_ref[at:at + rows, half * 128:half * 128 + 128] = final[p].astype(jnp.float32)

    loop(1, nblk, lambda d: gather(d).wait_send())
    loop(1, nrep, lambda e: scatter(e).wait_send())
    loop(1, nrep, lambda e: share(e).wait_send())
    loop(1, nblk, lambda d: across(d).wait_send())
    loop(1, nrep, lambda e: spread(e).wait_send())


def body(grad_out, relu_bits, features, weight, tiles, tile_rows, tile_counts):
    nblk = lax.axis_size("blk")
    nrep = lax.axis_size("rep")
    rows, width = grad_out.shape
    depth = features.shape[1]
    slots = tiles.shape[2]
    rows_share = depth * width // (nrep * 128)
    low, high = jnp.bfloat16, jnp.float32
    vmem = pl.BlockSpec(memory_space=pltpu.VMEM)
    smem = pl.BlockSpec(memory_space=pltpu.SMEM)
    dma = pltpu.SemaphoreType.DMA
    return pl.pallas_call(
        functools.partial(kernel, nblk, nrep, float(rows * nrep * nblk) ** -0.5),
        out_shape=(
            jax.ShapeDtypeStruct((rows, depth), low),
            jax.ShapeDtypeStruct((depth, width), high),
        ),
        in_specs=[smem, smem, vmem, vmem, vmem, vmem, vmem],
        out_specs=(vmem, vmem),
        scratch_shapes=[
            pltpu.VMEM((nblk, rows, width), low),
            pltpu.VMEM((nblk, slots, tiles.shape[4], tiles.shape[3]), low),
            pltpu.VMEM((depth, rows), low),
            pltpu.VMEM((nrep, rows, width), low),
            pltpu.VMEM((nrep, rows, width), low),
            pltpu.VMEM((rows, width), high),
            pltpu.VMEM((nrep, rows_share, 128), high),
            pltpu.VMEM((nrep, rows_share, 128), low),
            pltpu.VMEM((nrep, rows_share, 128), low),
            pltpu.VMEM((nblk, rows_share, 128), low),
            pltpu.VMEM((nrep, rows_share, 128), low),
            dma((nblk,)), dma((nblk,)),
            dma((nrep,)), dma((nrep,)),
            dma((nrep,)), dma((nrep,)),
            dma((nblk,)), dma((nblk,)),
            dma((nrep,)), dma((nrep,)),
        ],
        compiler_params=pltpu.CompilerParams(
            collective_id=0, has_side_effects=True, vmem_limit_bytes=40 * 1024 * 1024
        ),
        cost_estimate=pl.CostEstimate(flops=10**9, bytes_accessed=10**6, transcendentals=0),
    )(tile_rows, tile_counts, grad_out, relu_bits, features, weight, tiles)


def solution(mesh):
    return jax.shard_map(
        body,
        mesh=mesh,
        in_specs=(
            P(("blk", "rep"), None),
            P(("blk", "rep"), None),
            P(("blk", "rep"), None),
            P(),
            P(("blk", "rep"), None, None, None, None),
            P(("blk", "rep"), None, None),
            P(("blk", "rep"), None),
        ),
        out_specs=(P(("blk", "rep"), None), P()),
        check_vma=False,
    )
```

```python
import functools

import jax
import jax.numpy as jnp
from jax import lax
from jax.experimental import pallas as pl
from jax.experimental.pallas import tpu as pltpu
from jax.sharding import PartitionSpec as P

MESH = pl.DeviceIdType.MESH
UNROLL = 8
GROUP = 4


def loop(low, high, step):
    if high - low <= UNROLL:
        for index in range(low, high):
            step(index)
    else:
        lax.fori_loop(low, high, lambda index, carry: (step(index), carry)[1], 0)


def fold(count, step, start):
    if count <= UNROLL:
        for index in range(count):
            start = step(index, start)
        return start
    return lax.fori_loop(0, count, step, start)


def remote(source, target, send, receive, device):
    return pltpu.make_async_remote_copy(
        src_ref=source,
        dst_ref=target,
        send_sem=send,
        recv_sem=receive,
        device_id=device,
        device_id_type=MESH,
    )


def kernel(
    nblk, nrep, scale,
    rows_hbm, counts_hbm, grad_hbm, relu_hbm, feat_hbm, weight_hbm, tiles_hbm,
    gf_ref, gw_ref,
    rows_ref, counts_ref, grad_ref, relu_ref, feat_ref, weight_ref, tiles_ref, inputs,
    pieces, turned, feat_t, away, arrived, kept, mixed, gathered, own,
    terms, terms_low, share_in, block_sum, block_low, part_in, final,
    gs, gr, ps, pr, rs, rr, ts, tr, bs, br, ks, kr, fs, fr,
):
    me_b = lax.axis_index("blk")
    me_r = lax.axis_index("rep")
    slot_count = tiles_ref.shape[2]
    rows = terms.shape[1]
    halves = gw_ref.shape[1] // 128
    per_half = nblk // halves
    outer = nrep // 2
    me_o, me_i = me_r // 2, lax.rem(me_r, 2)

    barrier = pltpu.get_barrier_semaphore()

    def greet_b(d):
        pl.semaphore_signal(barrier, inc=1, device_id={"blk": lax.rem(me_b + d, nblk)}, device_id_type=MESH)

    def greet_r(e):
        pl.semaphore_signal(barrier, inc=1, device_id={"rep": lax.rem(me_r + e, nrep)}, device_id_type=MESH)

    loop(1, nrep, greet_r)
    loop(1, nblk, greet_b)
    order = (
        (grad_hbm, grad_ref), (relu_hbm, relu_ref), (tiles_hbm, tiles_ref), (rows_hbm, rows_ref),
        (counts_hbm, counts_ref), (feat_hbm, feat_ref), (weight_hbm, weight_ref),
    )
    load = [pltpu.make_async_copy(there, here, inputs.at[i]) for i, (there, here) in enumerate(order)]
    for copy in load:
        copy.start()
    load[0].wait()
    load[1].wait()
    grad = grad_ref[...]
    pieces[0] = jnp.where(relu_ref[...] == 1, grad, jnp.zeros_like(grad))
    pl.semaphore_wait(barrier, nblk + nrep - 2)

    def gather(d):
        return remote(pieces.at[0], pieces.at[d], gs.at[d], gr.at[d], {"blk": lax.rem(me_b + d, nblk)})

    loop(1, nblk, lambda d: gather(d).start())

    load[2].wait()

    def turn(d):
        source = lax.rem(me_b - d + nblk, nblk)
        for k in range(slot_count):
            turned[d, k] = tiles_ref[0, source, k].T

    loop(0, nblk, turn)
    for copy in load[3:]:
        copy.wait()
    feat_t[...] = feat_ref[...].T
    loop(1, nblk, lambda d: gather(d).wait_recv())

    def partial(t):
        def part(g, total):
            right = pieces[pl.ds(g * GROUP, GROUP)].reshape(GROUP * pieces.shape[1], pieces.shape[2])
            for k in range(slot_count):
                left = []
                for i in range(GROUP):
                    d = g * GROUP + i
                    source = lax.rem(me_b - d + nblk, nblk)
                    live = (rows_ref[0, k, source] == t) & (k < counts_ref[0, source])
                    here = turned[d, k]
                    gate = jnp.full((1, here.shape[1]), live.astype(jnp.float32)).astype(here.dtype)
                    left.append(here * gate)
                total = total + jnp.dot(jnp.concatenate(left, axis=1), right, preferred_element_type=jnp.float32)
            return total

        return fold(nblk // GROUP, part, jnp.zeros(own.shape, jnp.float32))

    def flip(q):
        total, bit = 0, 1
        while bit < outer:
            total = total + lax.rem(me_o // bit + q // bit, 2) * bit
            bit *= 2
        return total

    def pair(q):
        return remote(away.at[q], arrived.at[q], ps.at[q], pr.at[q], {"rep": me_o * 2 + 1 - me_i})

    def scatter(q):
        return remote(mixed.at[q], gathered.at[q], rs.at[q], rr.at[q], {"rep": flip(q) * 2 + me_i})

    def send_pair(step):
        q = outer - 1 - step
        away[q] = partial(flip(q) * 2 + 1 - me_i).astype(away.dtype)
        pair(q).start()
        kept[q] = partial(flip(q) * 2 + me_i)

    loop(0, outer, send_pair)

    def send_part(step):
        q = outer - 1 - step
        pair(q).wait_recv()
        mixed[q] = (kept[q] + arrived[q].astype(jnp.float32)).astype(mixed.dtype)
        scatter(q).start()

    loop(0, outer - 1, send_part)
    pair(0).wait_recv()
    own[...] = kept[0] + arrived[0].astype(jnp.float32)

    def take(step):
        q = step + 1
        scatter(q).wait_recv()
        own[...] += gathered[q].astype(jnp.float32)

    loop(0, outer - 1, take)
    aggregated = own[...].astype(jnp.bfloat16)

    term = jnp.dot(feat_t[...], aggregated, preferred_element_type=jnp.float32) * scale
    for p in range(nblk):
        half, at = p // per_half, (p % per_half) * rows
        cut = term[at:at + rows, half * 128:half * 128 + 128]
        terms[p] = cut
        terms_low[p] = cut.astype(terms_low.dtype)

    def share(d):
        other = lax.rem(me_b + d, nblk)
        return remote(terms_low.at[other], share_in.at[d], ts.at[d], tr.at[d], {"blk": other})

    loop(1, nblk, lambda d: share(d).start())
    gf_ref[...] = lax.dot_general(
        aggregated, weight_ref[...], (((1,), (1,)), ((), ())), preferred_element_type=jnp.float32
    ).astype(gf_ref.dtype)

    def take_share(index, total):
        share(index + 1).wait_recv()
        return total + share_in[index + 1].astype(jnp.float32)

    block_sum[...] = fold(nblk - 1, take_share, terms[me_b])
    part_rows = part_in.shape[1]
    split = part_rows < rows
    if split:
        block_low[...] = block_sum[...].astype(block_low.dtype)
        mine = pl.ds(pl.multiple_of(me_r * part_rows, part_rows), part_rows)

        def across(e):
            other = lax.rem(me_r + e, nrep)
            theirs = pl.ds(pl.multiple_of(other * part_rows, part_rows), part_rows)
            return remote(block_low.at[theirs], part_in.at[e], bs.at[e], br.at[e], {"rep": other})

        def take_part(index, total):
            across(index + 1).wait_recv()
            return total + part_in[index + 1].astype(jnp.float32)

        loop(1, nrep, lambda e: across(e).start())
        final[me_b, mine] = fold(nrep - 1, take_part, block_sum[mine]).astype(final.dtype)

        def regain(e):
            place = final.at[me_b, mine]
            return remote(place, place, ks.at[e], kr.at[e], {"rep": lax.rem(me_r + e, nrep)})

        loop(1, nrep, lambda e: regain(e).start())
        loop(1, nrep, lambda e: regain(e).wait_recv())
    else:
        part_in[me_r] = block_sum[...].astype(part_in.dtype)

        def across(e):
            place = part_in.at[me_r]
            return remote(place, place, bs.at[e], br.at[e], {"rep": lax.rem(me_r + e, nrep)})

        loop(1, nrep, lambda e: across(e).start())
        loop(1, nrep, lambda e: across(e).wait_recv())
        final[me_b] = fold(
            nrep, lambda r, total: total + part_in[r].astype(jnp.float32), jnp.zeros(block_sum.shape, jnp.float32)
        ).astype(final.dtype)

    def spread(d):
        return remote(final.at[me_b], final.at[me_b], fs.at[d], fr.at[d], {"blk": lax.rem(me_b + d, nblk)})

    loop(1, nblk, lambda d: spread(d).start())
    loop(1, nblk, lambda d: spread(d).wait_recv())
    for p in range(nblk):
        half, at = p // per_half, (p % per_half) * rows
        gw_ref[at:at + rows, half * 128:half * 128 + 128] = final[p].astype(jnp.float32)

    loop(1, nblk, lambda d: gather(d).wait_send())
    loop(0, outer, lambda q: pair(q).wait_send())
    loop(1, outer, lambda q: scatter(q).wait_send())
    loop(1, nblk, lambda d: share(d).wait_send())
    loop(1, nrep, lambda e: across(e).wait_send())
    if split:
        loop(1, nrep, lambda e: regain(e).wait_send())
    loop(1, nblk, lambda d: spread(d).wait_send())


def body(grad_out, relu_bits, features, weight, tiles, tile_rows, tile_counts):
    nblk = lax.axis_size("blk")
    nrep = lax.axis_size("rep")
    rows, width = grad_out.shape
    depth = features.shape[1]
    slots = tiles.shape[2]
    rows_share = depth * width // (nblk * 128)
    outer = nrep // 2
    rows_part = rows_share // nrep if rows_share % (16 * nrep) == 0 else rows_share
    low, high = jnp.bfloat16, jnp.float32
    vmem = pl.BlockSpec(memory_space=pltpu.VMEM)
    hbm = pl.BlockSpec(memory_space=pltpu.HBM)
    dma = pltpu.SemaphoreType.DMA
    return pl.pallas_call(
        functools.partial(kernel, nblk, nrep, float(rows * nrep * nblk) ** -0.5),
        out_shape=(
            jax.ShapeDtypeStruct((rows, depth), low),
            jax.ShapeDtypeStruct((depth, width), high),
        ),
        in_specs=[hbm] * 7,
        out_specs=(vmem, vmem),
        scratch_shapes=[
            pltpu.SMEM((1, slots, nblk), jnp.int32),
            pltpu.SMEM((1, nblk), jnp.int32),
            pltpu.VMEM((rows, width), low),
            pltpu.VMEM((rows, width), jnp.int32),
            pltpu.VMEM((rows, depth), low),
            pltpu.VMEM((depth, width), low),
            pltpu.VMEM(tiles.shape, low),
            dma((7,)),
            pltpu.VMEM((nblk, rows, width), low),
            pltpu.VMEM((nblk, slots, tiles.shape[4], tiles.shape[3]), low),
            pltpu.VMEM((depth, rows), low),
            pltpu.VMEM((outer, rows, width), low),
            pltpu.VMEM((outer, rows, width), low),
            pltpu.VMEM((outer, rows, width), high),
            pltpu.VMEM((outer, rows, width), low),
            pltpu.VMEM((outer, rows, width), low),
            pltpu.VMEM((rows, width), high),
            pltpu.VMEM((nblk, rows_share, 128), high),
            pltpu.VMEM((nblk, rows_share, 128), low),
            pltpu.VMEM((nblk, rows_share, 128), low),
            pltpu.VMEM((rows_share, 128), high),
            pltpu.VMEM((rows_share, 128), low),
            pltpu.VMEM((nrep, rows_part, 128), low),
            pltpu.VMEM((nblk, rows_share, 128), low),
            dma((nblk,)), dma((nblk,)),
            dma((outer,)), dma((outer,)),
            dma((outer,)), dma((outer,)),
            dma((nblk,)), dma((nblk,)),
            dma((nrep,)), dma((nrep,)),
            dma((nrep,)), dma((nrep,)),
            dma((nblk,)), dma((nblk,)),
        ],
        compiler_params=pltpu.CompilerParams(
            collective_id=0, has_side_effects=True, vmem_limit_bytes=64 * 1024 * 1024 - 65536
        ),
        cost_estimate=pl.CostEstimate(flops=10**9, bytes_accessed=10**6, transcendentals=0),
    )(jnp.swapaxes(tile_rows, 1, 2), tile_counts, grad_out, relu_bits, features, weight, tiles)


def solution(mesh):
    return jax.shard_map(
        body,
        mesh=mesh,
        in_specs=(
            P(("blk", "rep"), None),
            P(("blk", "rep"), None),
            P(("blk", "rep"), None),
            P(),
            P(("blk", "rep"), None, None, None, None),
            P(("blk", "rep"), None, None),
            P(("blk", "rep"), None),
        ),
        out_specs=(P(("blk", "rep"), None), P()),
        check_vma=False,
    )
```

```python
import functools

import jax
import jax.numpy as jnp
from jax import lax
from jax.experimental import pallas as pl
from jax.experimental.pallas import tpu as pltpu
from jax.sharding import PartitionSpec as P

MESH = pl.DeviceIdType.MESH
UNROLL = 8
GROUP = 4


def loop(low, high, step):
    if high - low <= UNROLL:
        for index in range(low, high):
            step(index)
    else:
        lax.fori_loop(low, high, lambda index, carry: (step(index), carry)[1], 0)


def fold(count, step, start):
    if count <= UNROLL:
        for index in range(count):
            start = step(index, start)
        return start
    return lax.fori_loop(0, count, step, start)


def remote(source, target, send, receive, device):
    return pltpu.make_async_remote_copy(
        src_ref=source,
        dst_ref=target,
        send_sem=send,
        recv_sem=receive,
        device_id=device,
        device_id_type=MESH,
    )


def flip(index, mask, count):
    total, bit = 0, 1
    while bit < count:
        total = total + lax.rem(index // bit + mask // bit, 2) * bit
        bit *= 2
    return total


def kernel(
    nblk, nrep, scale,
    rows_hbm, counts_hbm, grad_hbm, relu_hbm, feat_hbm, weight_hbm, tiles_hbm,
    gf_ref, gw_ref,
    rows_ref, counts_ref, grad_ref, relu_ref, feat_ref, weight_ref, tiles_ref, inputs,
    pieces, turned, feat_t, away, arrived, kept, mixed, gathered, own,
    terms, terms_low, share_in, block_sum, part_in, final,
    gs, gr, ps, pr, rs, rr, ts, tr, bs, br, fs, fr,
):
    me_b = lax.axis_index("blk")
    me_r = lax.axis_index("rep")
    slot_count = tiles_ref.shape[2]
    rows = terms.shape[1]
    halves = weight_hbm.shape[1] // 128
    per_half = nblk // halves
    outer = nrep // 2
    me_o, me_i = me_r // 2, lax.rem(me_r, 2)

    barrier = pltpu.get_barrier_semaphore()

    def greet_b(d):
        pl.semaphore_signal(barrier, inc=1, device_id={"blk": lax.rem(me_b + d, nblk)}, device_id_type=MESH)

    def greet_r(e):
        pl.semaphore_signal(barrier, inc=1, device_id={"rep": lax.rem(me_r + e, nrep)}, device_id_type=MESH)

    loop(1, nrep, greet_r)
    loop(1, nblk, greet_b)
    order = (
        (grad_hbm, grad_ref), (relu_hbm, relu_ref), (tiles_hbm, tiles_ref), (rows_hbm, rows_ref),
        (counts_hbm, counts_ref), (feat_hbm, feat_ref), (weight_hbm, weight_ref),
    )
    load = [pltpu.make_async_copy(there, here, inputs.at[i]) for i, (there, here) in enumerate(order)]
    for copy in load:
        copy.start()
    load[0].wait()
    load[1].wait()
    grad = grad_ref[...]
    pieces[0] = jnp.where(relu_ref[...] == 1, grad, jnp.zeros_like(grad))
    pl.semaphore_wait(barrier, nblk + nrep - 2)

    def gather(d):
        return remote(pieces.at[0], pieces.at[d], gs.at[d], gr.at[d], {"blk": lax.rem(me_b + d, nblk)})

    loop(1, nblk, lambda d: gather(d).start())

    load[2].wait()

    def turn(d):
        source = lax.rem(me_b - d + nblk, nblk)
        for k in range(slot_count):
            turned[d, k] = tiles_ref[0, source, k].T

    loop(0, nblk, turn)
    for copy in load[3:]:
        copy.wait()
    feat_t[...] = feat_ref[...].T
    loop(1, nblk, lambda d: gather(d).wait_recv())

    def partial(t):
        def part(g, total):
            right = pieces[pl.ds(g * GROUP, GROUP)].reshape(GROUP * pieces.shape[1], pieces.shape[2])
            for k in range(slot_count):
                left = []
                for i in range(GROUP):
                    d = g * GROUP + i
                    source = lax.rem(me_b - d + nblk, nblk)
                    live = (rows_ref[0, k, source] == t) & (k < counts_ref[0, source])
                    here = turned[d, k]
                    gate = jnp.full((1, here.shape[1]), live.astype(jnp.float32)).astype(here.dtype)
                    left.append(here * gate)
                total = total + jnp.dot(jnp.concatenate(left, axis=1), right, preferred_element_type=jnp.float32)
            return total

        return fold(nblk // GROUP, part, jnp.zeros(own.shape, jnp.float32))

    def pair(q):
        return remote(away.at[q], arrived.at[q], ps.at[q], pr.at[q], {"rep": me_o * 2 + 1 - me_i})

    def scatter(q):
        return remote(mixed.at[q], gathered.at[q], rs.at[q], rr.at[q], {"rep": flip(me_o, q, outer) * 2 + me_i})

    def send_pair(step):
        q = outer - 1 - step
        away[q] = partial(flip(me_o, q, outer) * 2 + 1 - me_i).astype(away.dtype)
        pair(q).start()
        kept[q] = partial(flip(me_o, q, outer) * 2 + me_i)

    loop(0, outer, send_pair)

    def send_part(step):
        q = outer - 1 - step
        pair(q).wait_recv()
        mixed[q] = (kept[q] + arrived[q].astype(jnp.float32)).astype(mixed.dtype)
        scatter(q).start()

    loop(0, outer - 1, send_part)
    pair(0).wait_recv()
    own[...] = kept[0] + arrived[0].astype(jnp.float32)

    def take(step):
        q = step + 1
        scatter(q).wait_recv()
        own[...] += gathered[q].astype(jnp.float32)

    loop(0, outer - 1, take)
    aggregated = own[...].astype(jnp.bfloat16)

    term = jnp.dot(feat_t[...], aggregated, preferred_element_type=jnp.float32) * scale
    for p in range(nblk):
        half, at = p // per_half, (p % per_half) * rows
        cut = term[at:at + rows, half * 128:half * 128 + 128]
        terms[p] = cut
        terms_low[p] = cut.astype(terms_low.dtype)

    def share(d):
        other = lax.rem(me_b + d, nblk)
        return remote(terms_low.at[other], share_in.at[d], ts.at[d], tr.at[d], {"blk": other})

    loop(1, nblk, lambda d: share(d).start())
    gf_ref[...] = lax.dot_general(
        aggregated, weight_ref[...], (((1,), (1,)), ((), ())), preferred_element_type=jnp.float32
    ).astype(gf_ref.dtype)

    def take_share(index, total):
        share(index + 1).wait_recv()
        return total + share_in[index + 1].astype(jnp.float32)

    block_sum[...] = fold(nblk - 1, take_share, terms[me_b])
    part_in[me_r] = block_sum[...].astype(part_in.dtype)

    def across(e):
        place = part_in.at[me_r]
        return remote(place, place, bs.at[e], br.at[e], {"rep": lax.rem(me_r + e, nrep)})

    loop(1, nrep, lambda e: across(e).start())
    loop(1, nrep, lambda e: across(e).wait_recv())
    final[me_b] = fold(
        nrep, lambda r, total: total + part_in[r].astype(jnp.float32), jnp.zeros(block_sum.shape, jnp.float32)
    ).astype(final.dtype)

    def spread(d):
        return remote(final.at[me_b], final.at[me_b], fs.at[d], fr.at[d], {"blk": lax.rem(me_b + d, nblk)})

    loop(1, nblk, lambda d: spread(d).start())
    loop(1, nblk, lambda d: spread(d).wait_recv())
    gw_ref[...] = final[...]

    loop(1, nblk, lambda d: gather(d).wait_send())
    loop(0, outer, lambda q: pair(q).wait_send())
    loop(1, outer, lambda q: scatter(q).wait_send())
    loop(1, nblk, lambda d: share(d).wait_send())
    loop(1, nrep, lambda e: across(e).wait_send())
    loop(1, nblk, lambda d: spread(d).wait_send())


def body(grad_out, relu_bits, features, weight, tiles, tile_rows, tile_counts):
    nblk = lax.axis_size("blk")
    nrep = lax.axis_size("rep")
    rows, width = grad_out.shape
    depth = features.shape[1]
    slots = tiles.shape[2]
    rows_share = depth * width // (nblk * 128)
    outer = nrep // 2
    low, high = jnp.bfloat16, jnp.float32
    vmem = pl.BlockSpec(memory_space=pltpu.VMEM)
    hbm = pl.BlockSpec(memory_space=pltpu.HBM)
    dma = pltpu.SemaphoreType.DMA
    grad_features, pieces = pl.pallas_call(
        functools.partial(kernel, nblk, nrep, float(rows * nrep * nblk) ** -0.5),
        out_shape=(
            jax.ShapeDtypeStruct((rows, depth), low),
            jax.ShapeDtypeStruct((nblk, rows_share, 128), low),
        ),
        in_specs=[hbm] * 7,
        out_specs=(vmem, vmem),
        scratch_shapes=[
            pltpu.SMEM((1, slots, nblk), jnp.int32),
            pltpu.SMEM((1, nblk), jnp.int32),
            pltpu.VMEM((rows, width), low),
            pltpu.VMEM((rows, width), jnp.int32),
            pltpu.VMEM((rows, depth), low),
            pltpu.VMEM((depth, width), low),
            pltpu.VMEM(tiles.shape, low),
            dma((7,)),
            pltpu.VMEM((nblk, rows, width), low),
            pltpu.VMEM((nblk, slots, tiles.shape[4], tiles.shape[3]), low),
            pltpu.VMEM((depth, rows), low),
            pltpu.VMEM((outer, rows, width), low),
            pltpu.VMEM((outer, rows, width), low),
            pltpu.VMEM((outer, rows, width), high),
            pltpu.VMEM((outer, rows, width), low),
            pltpu.VMEM((outer, rows, width), low),
            pltpu.VMEM((rows, width), high),
            pltpu.VMEM((nblk, rows_share, 128), high),
            pltpu.VMEM((nblk, rows_share, 128), low),
            pltpu.VMEM((nblk, rows_share, 128), low),
            pltpu.VMEM((rows_share, 128), high),
            pltpu.VMEM((nrep, rows_share, 128), low),
            pltpu.VMEM((nblk, rows_share, 128), low),
            dma((nblk,)), dma((nblk,)),
            dma((outer,)), dma((outer,)),
            dma((outer,)), dma((outer,)),
            dma((nblk,)), dma((nblk,)),
            dma((nrep,)), dma((nrep,)),
            dma((nblk,)), dma((nblk,)),
        ],
        compiler_params=pltpu.CompilerParams(
            collective_id=0, has_side_effects=True, vmem_limit_bytes=64 * 1024 * 1024 - 65536
        ),
        cost_estimate=pl.CostEstimate(flops=10**9, bytes_accessed=10**6, transcendentals=0),
    )(jnp.swapaxes(tile_rows, 1, 2), tile_counts, grad_out, relu_bits, features, weight, tiles)
    halves = width // 128
    stacked = pieces.reshape(halves, depth, 128)
    grad_weight = jnp.swapaxes(stacked, 0, 1).reshape(depth, width).astype(high)
    return grad_features, grad_weight


def solution(mesh):
    return jax.shard_map(
        body,
        mesh=mesh,
        in_specs=(
            P(("blk", "rep"), None),
            P(("blk", "rep"), None),
            P(("blk", "rep"), None),
            P(),
            P(("blk", "rep"), None, None, None, None),
            P(("blk", "rep"), None, None),
            P(("blk", "rep"), None),
        ),
        out_specs=(P(("blk", "rep"), None), P()),
        check_vma=False,
    )
```
